1024 devices in a mesh: tm: 8 (over x), height: 16 (over z, core), expert: 8 (over y).
Axes of the slice: x: 8, y: 8, z: 8, core: 2. Of those that a mesh axis runs over, the one named last changes fastest.
Arguments:
- saved_conv: bfloat16 [32, 64, 16, 4096], P('tm', 'height', None, 'expert'), may hold values from -6 to 6
- grad_out: bfloat16 [32, 64, 16, 4096], P('tm', 'height', None, 'expert'), may hold values from -1.5 to 1.5
- conv_kernel: float32 [27, 4096], P(None, 'expert'), may hold values from -1 to 1
- weight_in: bfloat16 [8, 4096, 2048], P(None, 'expert', 'height'), may hold values from -0.09375 to 0.09375
- weight_out: bfloat16 [8, 2048, 4096], P(None, 'height', 'expert'), may hold values from -0.125 to 0.125
- gate_values: float32 [8, 8, 256], P('tm'), may hold values from 0.2 to 1
- picked_slots: int32 [8, 16, 8, 16], P('tm', 'height'), may hold values from 0 to 255, as said below
- slot_counts: int32 [8, 16, 8], P('tm', 'height'), may hold values from 0 to 16, as said below
Outputs:
- grad_input: float32 [32, 64, 16, 4096], P('tm', 'height', None, 'expert')
- grad_weight_in: float32 [8, 4096, 2048], P('tm', 'expert', 'height')
- grad_weight_out: float32 [8, 2048, 4096], P('tm', 'height', 'expert')
The draws below stay inside these ranges and needn't reach their ends.
Inputs may be any that keep to these rules, and one draw needn't show every extreme that they name: `picked_slots`: the 16 indices of one expert for one frame block and row block are distinct; slots at or past the count are ignored. `slot_counts`: one expert has all 16 slots live for every frame block and row block.
All inputs are finite; a program needn't handle non-finite values.
Results may differ from the reference program's by a relative error of at most 0.015.
Values may be sent and summed in bfloat16 or wider, within the bound.
A program may use at most 64 MiB of HBM per device.

```python
import jax
import jax.numpy as jnp
from jax import lax

D = 4096
HID = 2048
COLS = 16
SLOT = 16
TOK_DEV = 256
EXPERTS = 8
CAP = 256
NF = 32
NR = 64
N_TM = 8
N_HEIGHT = 16


def draw_picked_slots(key, part):
    key = jax.random.fold_in(key, 11)
    scores = jax.random.randint(key, (N_TM, N_HEIGHT, EXPERTS, TOK_DEV), 0, 2 ** 31 // TOK_DEV - 1)
    scores = scores * TOK_DEV + jnp.arange(TOK_DEV, dtype=jnp.int32)
    ranking = jnp.argsort(scores, axis=-1).astype(jnp.int32)
    return ranking[..., :SLOT]


def draw_slot_counts(key, part):
    key = jax.random.fold_in(key, 23)
    key_count, key_full = jax.random.split(key)
    counts = jax.random.randint(key_count, (N_TM, N_HEIGHT, EXPERTS), 0, SLOT + 1)
    full_expert = jax.random.randint(key_full, (), 0, EXPERTS)
    chosen = jnp.arange(EXPERTS, dtype=jnp.int32)[None, None, :] == full_expert
    return jnp.where(chosen, SLOT, counts).astype(jnp.int32)


def block_levels(own_key, shape, shards, smallest, largest):
    loudness = 1.0
    for axis_at, blocks in shards:
        heights = jax.random.uniform(jax.random.fold_in(jax.random.fold_in(own_key, 6), axis_at), (blocks,), jnp.float32, smallest / len(shards), largest / len(shards))
        loudness = loudness * jnp.repeat(jnp.exp(heights), shape[axis_at] // blocks).reshape((-1,) + (1,) * (len(shape) - 1 - axis_at))
    return loudness


def centred(stream_key, dims, deviation, reach, shards=(), kind=jnp.bfloat16):
    drawn = deviation * jax.random.normal(stream_key, dims, jnp.float32)
    if shards:
        drawn = drawn * block_levels(stream_key, dims, shards, -0.22, 0.18)
    return jnp.clip(drawn, -reach, reach).astype(kind)


def setup_inputs(seed: int = 0) -> dict:
    key_of = jax.random.split(jax.random.key(seed), 9)
    saved_conv = centred(key_of[0], (NF, NR, COLS, D), 1.0, 6.0, ((0, 8), (1, 16), (3, 8)))
    grad_out = centred(key_of[1], (NF, NR, COLS, D), 0.25, 1.5, ((0, 8), (1, 16), (3, 8)))
    conv_kernel = centred(key_of[2], (27, D), 0.2, 1.0, ((1, 8),), jnp.float32)
    weight_in = centred(key_of[3], (EXPERTS, D, HID), D ** -0.5, 0.09375, ((1, 8), (2, 16)))
    weight_out = centred(key_of[4], (EXPERTS, HID, D), HID ** -0.5, 0.125, ((1, 16), (2, 8)))
    gate_values = jnp.clip(0.2 + 0.8 * jax.random.uniform(key_of[5], (N_TM, EXPERTS, CAP), jnp.float32) ** block_levels(key_of[5], (N_TM, EXPERTS, CAP), ((0, 8),), -0.2, 0.2), 0.2, 1.0)
    picked_slots = draw_picked_slots(jax.random.fold_in(key_of[8], 71), 0)
    slot_counts = draw_slot_counts(jax.random.fold_in(key_of[8], 71), 0)
    return {"saved_conv": saved_conv, "grad_out": grad_out, "conv_kernel": conv_kernel, "weight_in": weight_in, "weight_out": weight_out, "gate_values": gate_values, "picked_slots": picked_slots, "slot_counts": slot_counts}


def smooth_gate(value):
    return jax.nn.gelu(value, approximate=True)

def round_half(value):
    return lax.optimization_barrier(value.astype(jnp.bfloat16)).astype(jnp.float32)

def transpose_conv(field_half, conv_kernel):
    frames, grid_rows, grid_cols, model_width = field_half.shape
    padded = jnp.pad(field_half, ((1, 1), (1, 1), (1, 1), (0, 0)))
    total = jnp.zeros(field_half.shape, jnp.float32)
    for offset_f in range(3):
        for offset_r in range(3):
            for offset_c in range(3):
                kernel_row = conv_kernel[offset_f * 9 + offset_r * 3 + offset_c]
                window = padded[2 - offset_f:2 - offset_f + frames, 2 - offset_r:2 - offset_r + grid_rows, 2 - offset_c:2 - offset_c + grid_cols]
                total = total + kernel_row * window.astype(jnp.float32)
    return total

def reference(saved_conv, grad_out, conv_kernel, weight_in, weight_out, gate_values, picked_slots, slot_counts):
    frames, grid_rows, grid_cols, model_width = saved_conv.shape
    frames_dev = frames // N_TM
    rows_dev = grid_rows // N_HEIGHT
    hidden = weight_in.shape[2]
    tm_pos = jnp.arange(N_TM, dtype=jnp.int32)[:, None, None, None]
    ht_pos = jnp.arange(N_HEIGHT, dtype=jnp.int32)[None, :, None, None]
    frame_at = tm_pos * frames_dev + picked_slots // (rows_dev * grid_cols)
    row_at = ht_pos * rows_dev + picked_slots // grid_cols % rows_dev
    col_at = picked_slots % grid_cols
    flat_index = ((frame_at * grid_rows + row_at) * grid_cols + col_at).astype(jnp.int32)
    slot_live = jnp.arange(SLOT, dtype=jnp.int32)[None, None, None, :] < slot_counts[..., None]
    order_index = jnp.transpose(flat_index, (0, 2, 1, 3)).reshape(N_TM, EXPERTS, CAP)
    order_live = jnp.transpose(slot_live, (0, 2, 1, 3)).reshape(N_TM, EXPERTS, CAP)
    flat_conv = saved_conv.reshape(-1, model_width)
    flat_grad = grad_out.reshape(-1, model_width)

    def one_expert(packed):
        slot_index, live_rows, gate_row, proj_in, proj_out = packed
        rows_conv = jnp.where(live_rows[:, None], flat_conv[slot_index], jnp.zeros((), jnp.bfloat16))
        rows_grad = jnp.where(live_rows[:, None], flat_grad[slot_index], jnp.zeros((), jnp.bfloat16))
        pre_full = jnp.dot(rows_conv, proj_in, preferred_element_type=jnp.float32)
        back_full = jnp.dot(rows_grad, proj_out.T, preferred_element_type=jnp.float32)
        activated = smooth_gate(pre_full).astype(jnp.bfloat16)
        _, pullback = jax.vjp(smooth_gate, pre_full)
        grad_pre = pullback(gate_row[:, None] * back_full)[0].astype(jnp.bfloat16)
        scaled_grad = (gate_row[:, None] * rows_grad.astype(jnp.float32)).astype(jnp.bfloat16)
        part_out = jnp.dot(activated.T, scaled_grad, preferred_element_type=jnp.float32)
        part_in = jnp.dot(rows_conv.T, grad_pre, preferred_element_type=jnp.float32)
        picked_grad = jnp.dot(grad_pre, proj_in.T, preferred_element_type=jnp.float32).astype(jnp.bfloat16)
        return (round_half(part_in), round_half(part_out), picked_grad)

    def group_step(carry, group):
        total_in, total_out = carry
        parts = lax.map(one_expert, (order_index[group], order_live[group], gate_values[group], weight_in, weight_out))
        return ((total_in + parts[0], total_out + parts[1]), parts[2])
    start_in = jnp.zeros((EXPERTS, model_width, hidden), jnp.float32)
    start_out = jnp.zeros((EXPERTS, hidden, model_width), jnp.float32)
    sums, picked_grads = lax.scan(group_step, (start_in, start_out), jnp.arange(N_TM, dtype=jnp.int32))
    grad_weight_in, grad_weight_out = sums
    masked = jnp.where(order_live[..., None], picked_grads, jnp.zeros((), jnp.bfloat16))
    field = flat_grad.astype(jnp.float32).at[order_index.reshape(-1)].add(masked.reshape(-1, model_width).astype(jnp.float32))
    field = field.reshape(frames, grid_rows, grid_cols, model_width)
    field_half = field.astype(jnp.bfloat16)
    grad_input = field + transpose_conv(field_half, conv_kernel)
    return (grad_input, grad_weight_in, grad_weight_out)
```

```python
import functools

import jax
import jax.numpy as jnp
from jax import lax
from jax.experimental import pallas as pl
from jax.experimental.pallas import tpu as pltpu
from jax.sharding import PartitionSpec as P

MESH = pl.DeviceIdType.MESH
HALF = jnp.bfloat16
FULL = jnp.float32


def near_first(count):
    order = [0]
    for step in range(1, count // 2):
        order += [step, count - step]
    return order + [count // 2]


def dot_nn(a, b):
    return lax.dot_general(a, b, (((1,), (0,)), ((), ())), preferred_element_type=FULL)


def dot_nt(a, b):
    return lax.dot_general(a, b, (((1,), (1,)), ((), ())), preferred_element_type=FULL)


def dot_tn(a, b):
    return lax.dot_general(a, b, (((0,), (0,)), ((), ())), preferred_element_type=FULL)


def gelu_and_slope(value):
    scale = 0.7978845608028654
    square = value * value
    tanh = jnp.tanh(scale * (value + 0.044715 * value * square))
    half_up = 0.5 * (1.0 + tanh)
    slope = half_up + 0.5 * value * (1.0 - tanh * tanh) * (
        scale * (1.0 + 3.0 * 0.044715 * square)
    )
    return value * half_up, slope


def body(
    nx, nh, ny,
    conv_ref, grad_ref, taps_ref, win_ref, wout_ref, gate_ref, slots_ref, counts_ref,
    out_ref, gin_ref, gout_ref,
    chosen, rows, w_in, w_out, part_to, part_from, hidden, picked,
    sum_to_r, sum_to_l, sum_from_r, sum_from_l, back_to, back_from,
    grads_own, grads_to, grads_from, field, rim, shifted,
    x_send, x_recv, w_own, w_send, w_recv, z_send, z_recv, p_send, p_recv,
    a_send, a_recv, s_send, s_recv, b_send, b_recv, g_send, g_recv, h_send, h_recv,
):
    nz = nh // 2
    x, h, y = lax.axis_index("tm"), lax.axis_index("height"), lax.axis_index("expert")
    tokens, width = conv_ref.shape
    slot = slots_ref.shape[1]
    picks = nx * slot
    units = win_ref.shape[2]
    x_order, z_order = near_first(nx), near_first(nz)
    x_at = {d: i for i, d in enumerate(x_order)}
    z_at = {d: i for i, d in enumerate(z_order)}
    partner = h + 1 - 2 * lax.rem(h, 2)
    right, left = lax.rem(h + 2, nh), lax.rem(h + nh - 2, nh)
    sides = [(a, b) for a in (-1, 0, 1) for b in (-1, 0, 1) if (a, b) != (0, 0)]

    def x_far(d):
        return lax.rem(x + d + nx, nx)

    def y_far(d):
        return lax.rem(y + d + ny, ny)

    def h_far(d):
        return lax.rem(h + d + nh, nh)

    pending = []

    def remote(src, dst, sems_to, sems_from, device):
        copy = pltpu.make_async_remote_copy(
            src_ref=src, dst_ref=dst, send_sem=sems_to, recv_sem=sems_from,
            device_id=device, device_id_type=MESH,
        )
        copy.start()
        pending.append(copy)
        return copy

    peers = [(x_far(d), h, y) for d in range(1, nx)]
    peers += [(x, h, y_far(d)) for d in range(1, ny)]
    peers += [(x, right, y), (x, left, y), (x, partner, y)]
    peers += [(x_far(a), h_far(b), y) for a, b in sides if b != 0]
    barrier = pltpu.get_barrier_semaphore()
    for peer in peers:
        pl.semaphore_signal(barrier, inc=1, device_id=peer, device_id_type=MESH)

    own_weights = [
        pltpu.make_async_copy(win_ref.at[x], w_in.at[:, pl.ds(0, units)], w_own.at[0]),
        pltpu.make_async_copy(wout_ref.at[x], w_out.at[pl.ds(0, units)], w_own.at[1]),
    ]
    for copy in own_weights:
        copy.start()

    lane = lax.broadcasted_iota(jnp.int32, (nx, picks), 1)
    expert_row = lax.broadcasted_iota(jnp.int32, (nx, picks), 0)
    mine = (lane // slot == expert_row).astype(FULL)
    spread_row = lax.broadcasted_iota(jnp.int32, (slot, picks), 0)
    spread_lane = lax.broadcasted_iota(jnp.int32, (slot, picks), 1)
    spread = (lax.rem(spread_lane, slot) == spread_row).astype(FULL)
    index_row = jnp.sum(
        mine * dot_nn(slots_ref[...].astype(FULL), spread), axis=0, keepdims=True
    )
    count_row = dot_nn(counts_ref[...].astype(FULL), mine)
    lane_row = lax.broadcasted_iota(jnp.int32, (1, picks), 1)
    live = lax.rem(lane_row, slot).astype(FULL) < count_row - 0.5
    index_row = jnp.where(live, index_row, -1.0)
    gate_row_at = lax.broadcasted_iota(jnp.int32, (nh * slot, picks), 0)
    gate_lane = lax.broadcasted_iota(jnp.int32, (nh * slot, picks), 1)
    gate_pick = (gate_row_at == h * slot + lax.rem(gate_lane, slot)).astype(FULL)
    gate_row = jnp.sum(
        mine
        * lax.dot_general(
            gate_ref[...], gate_pick, (((1,), (0,)), ((), ())),
            precision=lax.Precision.HIGHEST, preferred_element_type=FULL,
        ),
        axis=0,
        keepdims=True,
    )
    token = lax.broadcasted_iota(jnp.int32, (tokens, picks), 0).astype(FULL)
    selector = (token == index_row).astype(HALF)
    gates = jnp.transpose(jnp.broadcast_to(gate_row, (picks, picks)))
    gates = jnp.concatenate([gates] * (width // picks), axis=1)
    conv_rows = dot_tn(selector, conv_ref[...]).astype(HALF)
    grad_rows = (dot_tn(selector, grad_ref[...]) * gates).astype(HALF)
    chosen[:, 0] = conv_rows.reshape(nx, slot, width)
    chosen[:, 1] = grad_rows.reshape(nx, slot, width)
    rows[0, 0] = chosen[x]

    pl.semaphore_wait(barrier, len(peers))

    x_copies = {}
    for d in x_order[1:]:
        there = x_at[nx - d]
        x_copies[there] = remote(
            chosen.at[x_far(d)], rows.at[0, there], x_send.at[there], x_recv.at[there],
            (x_far(d), h, y),
        )
    weight_copies = [
        remote(win_ref.at[x], w_in.at[:, pl.ds(units, units)], w_send.at[0], w_recv.at[0],
               (x, partner, y)),
        remote(wout_ref.at[x], w_out.at[pl.ds(units, units)], w_send.at[1], w_recv.at[1],
               (x, partner, y)),
    ]

    split = nx // 2
    halves = (pl.ds(0, split), pl.ds(split, split))
    steps = nz // 2
    z_copies = {}

    def z_forward(step, part, way):
        source = (step - 1) if way == 1 else (nz - step + 1) % nz
        target = step if way == 1 else (nz - step) % nz
        key = ((step - 1) * 2 + part) * 2 + way
        z_copies[step, part, way] = remote(
            rows.at[z_at[source], halves[part]], rows.at[z_at[target], halves[part]],
            z_send.at[key], z_recv.at[key], (x, left if way == 1 else right, y),
        )

    def z_goes(step, part, way):
        return step < steps or (step == steps and part == way)

    for part in (0, 1):
        for there in range(part * split, (part + 1) * split):
            if there in x_copies:
                x_copies[there].wait_recv()
        for way in (0, 1):
            if z_goes(1, part, way):
                z_forward(1, part, way)

    for copy in own_weights:
        copy.wait()
    for copy in weight_copies:
        copy.wait_recv()

    p_copies = {}

    def partial_sums(stage, first, last):
        for block in range(first, last):
            conv_block = rows[block, :, 0].reshape(picks, width)
            grad_block = rows[block, :, 1].reshape(picks, width)
            part_to[:, block, 0] = dot_nn(conv_block, w_in[...]).astype(HALF).reshape(
                ny, slot, 2 * units)
            part_to[:, block, 1] = dot_nt(grad_block, w_out[...]).astype(HALF).reshape(
                ny, slot, 2 * units)
        span = pl.ds(first, last - first)
        for d in reversed(near_first(ny)[1:]):
            key = stage * ny + ny - d
            p_copies[stage, ny - d] = remote(
                part_to.at[y_far(d), span], part_from.at[ny - d, span],
                p_send.at[key], p_recv.at[key], (x, h, y_far(d)),
            )

    def own_hidden(stage, first, last):
        span = pl.ds(first, last - first)
        total = part_to[y, span].astype(FULL)
        for d in range(1, ny):
            p_copies[stage, d].wait_recv()
            total = total + part_from[d, span].astype(FULL)
        activated, slope = gelu_and_slope(total[:, 0])
        hidden[span, y, 0] = activated.astype(HALF)
        hidden[span, y, 1] = (slope * total[:, 1]).astype(HALF)

    spans = [(0, 1)] + [(2 * k - 1, 2 * k + 1) for k in range(1, steps)] + [(nz - 1, nz)]
    partial_sums(0, *spans[0])
    for step in range(1, steps + 1):
        for part in (0, 1):
            for way in (0, 1):
                if z_goes(step, part, way):
                    z_copies[step, part, way].wait_recv()
                    if step < steps and z_goes(step + 1, part, way):
                        z_forward(step + 1, part, way)
        partial_sums(step, *spans[step])
        own_hidden(step - 1, *spans[step - 1])
    own_hidden(steps, *spans[steps])

    y_steps = ny // 2
    blocks = (pl.ds(nz // 2, nz - nz // 2), pl.ds(0, nz // 2))
    a_copies = {}

    def a_forward(step, part, way):
        piece = y_far(step - 1) if way == 1 else y_far(1 - step)
        key = ((step - 1) * 2 + part) * 2 + way
        a_copies[step, part, way] = remote(
            hidden.at[blocks[part], piece], hidden.at[blocks[part], piece],
            a_send.at[key], a_recv.at[key], (x, h, y_far(-1) if way == 1 else y_far(1)),
        )

    def a_goes(step, part, way):
        return step < y_steps or (step == y_steps and part == way)

    for part in (0, 1):
        for way in (0, 1):
            if a_goes(1, part, way):
                a_forward(1, part, way)
    for step in range(1, y_steps + 1):
        for part in (0, 1):
            for way in (0, 1):
                if a_goes(step, part, way):
                    a_copies[step, part, way].wait_recv()
                    if step < y_steps and a_goes(step + 1, part, way):
                        a_forward(step + 1, part, way)

    def picked_block(block):
        grad_pre = hidden[block, :, 1].reshape(picks, 2 * units)
        picked[block] = dot_nt(grad_pre, w_in[...])

    middle = picks // 2
    lines = (pl.ds(0, middle), pl.ds(middle, middle))
    stage_to, stage_from = (sum_to_r, sum_to_l), (sum_from_r, sum_from_l)
    s_copies = {}

    def s_add(step, part, way):
        distance = steps + 1 - step
        block = z_at[distance if way == 0 else (nz - distance) % nz]
        total = picked[block, lines[part]]
        if (step - 1, part, way) in s_copies:
            s_copies[step - 1, part, way].wait_recv()
            total = total + stage_from[way][step - 2, lines[part]].astype(FULL)
        stage_to[way][step - 1, lines[part]] = total.astype(HALF)
        key = ((step - 1) * 2 + part) * 2 + way
        s_copies[step, part, way] = remote(
            stage_to[way].at[step - 1, lines[part]], stage_from[way].at[step - 1, lines[part]],
            s_send.at[key], s_recv.at[key], (x, left if way == 1 else right, y),
        )

    def weight_grads_out():
        activated = hidden[:, :, 0].reshape(nz * picks, 2 * units)
        grads = dot_tn(activated, rows[:, :, 1].reshape(nz * picks, width))
        gout_ref[...] = grads[:units]
        grads_to[0] = grads[units:]

    def weight_grads_in():
        grad_pre = hidden[:, :, 1].reshape(nz * picks, 2 * units)
        grads = dot_tn(grad_pre, rows[:, :, 0].reshape(nz * picks, width))
        grads_own[...] = grads[:units]
        grads_to[1] = grads[units:]

    picked_block(nz - 1)
    for way in (0, 1):
        s_add(1, way, way)
    for step in range(2, steps + 1):
        distance = steps + 1 - step
        for block in (z_at[distance], z_at[nz - distance]):
            picked_block(block)
        if step == steps:
            weight_grads_out()
        for part in (0, 1):
            for way in (0, 1):
                s_add(step, part, way)
    picked_block(0)
    for part in (0, 1):
        total = picked[0, lines[part]]
        for way in (0, 1):
            if (steps, part, way) in s_copies:
                s_copies[steps, part, way].wait_recv()
                total = total + stage_from[way][steps - 1, lines[part]].astype(FULL)
        back_to[pl.ds(part * split, split)] = total.astype(HALF).reshape(split, slot, width)

    b_copies = []
    for d in x_order[1:]:
        b_copies.append(
            remote(back_to.at[x_at[d]], back_from.at[x], b_send.at[d], b_recv.at[d],
                   (x_far(d), h, y))
        )
    back_from[x] = back_to[0]
    weight_grads_in()
    g_copy = remote(grads_to, grads_from, g_send, g_recv, (x, partner, y))
    for copy in b_copies:
        copy.wait_recv()
    added = dot_nn(selector, back_from[...].reshape(picks, width))
    total_field = grad_ref[...].astype(FULL) + added
    frames, grid_rows, columns, _ = out_ref.shape
    field[...] = total_field.reshape(frames, grid_rows, columns, width)
    rim[pl.ds(1, frames), pl.ds(1, grid_rows)] = total_field.astype(HALF).reshape(
        frames, grid_rows, columns, width)

    def face(side, size, inside):
        if side == 0:
            return pl.ds(1, size)
        if inside:
            return pl.ds(1 if side < 0 else size, 1)
        return pl.ds(size + 1 if side < 0 else 0, 1)

    h_copies = []
    for at, (a, b) in enumerate(sides):
        h_copies.append(
            remote(
                rim.at[face(a, frames, True), face(b, grid_rows, True)],
                rim.at[face(a, frames, False), face(b, grid_rows, False)],
                h_send.at[at], h_recv.at[at], (x_far(a), h_far(b), y),
            )
        )

    g_copy.wait_recv()
    gout_ref[...] += grads_from[0]
    gin_ref[...] = jnp.transpose(grads_own[...] + grads_from[1])

    for copy in h_copies:
        copy.wait_recv()

    at_column = lax.broadcasted_iota(jnp.int32, (columns, width), 0)

    def shift(cell, _):
        f, r = cell // (grid_rows + 2), lax.rem(cell, grid_rows + 2)
        outside = ((f == 0) & (x == 0)) | ((f == frames + 1) & (x == nx - 1))
        outside |= ((r == 0) & (h == 0)) | ((r == grid_rows + 1) & (h == nh - 1))
        here = jnp.where(outside, 0.0, rim[f, r].astype(FULL))
        shifted[1, f, r] = here
        shifted[0, f, r] = jnp.where(
            at_column == columns - 1, 0.0, pltpu.roll(here, columns - 1, 0))
        shifted[2, f, r] = jnp.where(at_column == 0, 0.0, pltpu.roll(here, 1, 0))
        return _

    lax.fori_loop(0, (frames + 2) * (grid_rows + 2), shift, 0)

    def convolve(f, _):
        total = field[f]
        for a in range(3):
            for b in range(3):
                for k in range(3):
                    tap = taps_ref[pl.ds(9 * a + 3 * b + k, 1)].reshape(1, 1, width)
                    total = total + tap * shifted[k, f + 2 - a, pl.ds(2 - b, grid_rows)]
        out_ref[f] = total
        return _

    lax.fori_loop(0, frames, convolve, 0)

    for copy in pending:
        copy.wait_send()


def on_device(
    nx, nh, ny,
    saved_conv, grad_out, conv_kernel, weight_in, weight_out, gate_values, picked_slots, slot_counts,
):
    nz = nh // 2
    frames, grid_rows, columns, width = saved_conv.shape
    tokens = frames * grid_rows * columns
    experts, _, units = weight_in.shape
    slot = picked_slots.shape[3]
    picks = experts * slot
    vmem = pl.BlockSpec(memory_space=pltpu.VMEM)
    hbm = pl.BlockSpec(memory_space=pl.ANY)
    steps = nz // 2
    dma = pltpu.SemaphoreType.DMA
    out, grad_in, grad_w = pl.pallas_call(
        functools.partial(body, nx, nh, ny),
        out_shape=(
            jax.ShapeDtypeStruct((frames, grid_rows, columns, width), FULL),
            jax.ShapeDtypeStruct((width, units), FULL),
            jax.ShapeDtypeStruct((units, width), FULL),
        ),
        in_specs=[vmem, vmem, vmem, hbm, hbm, vmem, vmem, vmem],
        out_specs=(vmem, vmem, vmem),
        scratch_shapes=[
            pltpu.VMEM((experts, 2, slot, width), HALF),
            pltpu.VMEM((nz, nx, 2, slot, width), HALF),
            pltpu.VMEM((width, 2 * units), HALF),
            pltpu.VMEM((2 * units, width), HALF),
            pltpu.VMEM((ny, nz, 2, slot, 2 * units), HALF),
            pltpu.VMEM((ny, nz, 2, slot, 2 * units), HALF),
            pltpu.VMEM((nz, ny, 2, slot, 2 * units), HALF),
            pltpu.VMEM((nz, picks, width), FULL),
            pltpu.VMEM((steps, picks, width), HALF),
            pltpu.VMEM((steps, picks, width), HALF),
            pltpu.VMEM((steps, picks, width), HALF),
            pltpu.VMEM((steps, picks, width), HALF),
            pltpu.VMEM((nx, slot, width), HALF),
            pltpu.VMEM((nx, slot, width), HALF),
            pltpu.VMEM((units, width), FULL),
            pltpu.VMEM((2, units, width), FULL),
            pltpu.VMEM((2, units, width), FULL),
            pltpu.VMEM((frames, grid_rows, columns, width), FULL),
            pltpu.VMEM((frames + 2, grid_rows + 2, columns, width), HALF),
            pltpu.VMEM((3, frames + 2, grid_rows + 2, columns, width), FULL),
            dma((nx,)), dma((nx,)),
            dma((2,)), dma((2,)), dma((2,)),
            dma((4 * steps,)), dma((4 * steps,)),
            dma(((steps + 1) * ny,)), dma(((steps + 1) * ny,)),
            dma((2 * ny,)), dma((2 * ny,)),
            dma((4 * steps,)), dma((4 * steps,)),
            dma((nx,)), dma((nx,)),
            dma(()), dma(()),
            dma((8,)), dma((8,)),
        ],
        compiler_params=pltpu.CompilerParams(
            collective_id=0, has_side_effects=True, vmem_limit_bytes=48 * 1024 * 1024
        ),
    )(
        saved_conv.reshape(tokens, width),
        grad_out.reshape(tokens, width),
        conv_kernel,
        weight_in,
        weight_out,
        gate_values.reshape(gate_values.shape[1:]),
        picked_slots.reshape(experts, slot),
        slot_counts.reshape(1, experts),
    )
    return out, grad_in[None], grad_w[None]


def solution(mesh):
    placed = (
        P("tm", "height", None, "expert"),
        P("tm", "height", None, "expert"),
        P(None, "expert"),
        P(None, "expert", "height"),
        P(None, "height", "expert"),
        P("tm", None, None),
        P("tm", "height", None, None),
        P("tm", "height", None),
    )
    sizes = (mesh.shape["tm"], mesh.shape["height"], mesh.shape["expert"])
    return jax.shard_map(
        functools.partial(on_device, *sizes),
        mesh=mesh,
        in_specs=placed,
        out_specs=(
            P("tm", "height", None, "expert"),
            P("tm", "expert", "height"),
            P("tm", "height", "expert"),
        ),
        check_vma=False,
    )
```

```python
import functools

import jax
import jax.numpy as jnp
from jax import lax
from jax.experimental import pallas as pl
from jax.experimental.pallas import tpu as pltpu
from jax.sharding import PartitionSpec as P

MESH = pl.DeviceIdType.MESH
HALF = jnp.bfloat16
FULL = jnp.float32


def near_first(count):
    order = [0]
    for step in range(1, count // 2):
        order += [step, count - step]
    return order + [count // 2]


def dot_nn(a, b):
    return lax.dot_general(a, b, (((1,), (0,)), ((), ())), preferred_element_type=FULL)


def dot_nt(a, b):
    return lax.dot_general(a, b, (((1,), (1,)), ((), ())), preferred_element_type=FULL)


def dot_tn(a, b):
    return lax.dot_general(a, b, (((0,), (0,)), ((), ())), preferred_element_type=FULL)


def gelu_and_slope(value):
    scale = 0.7978845608028654
    square = value * value
    tanh = jnp.tanh(scale * (value + 0.044715 * value * square))
    half_up = 0.5 * (1.0 + tanh)
    slope = half_up + 0.5 * value * (1.0 - tanh * tanh) * (
        scale * (1.0 + 3.0 * 0.044715 * square)
    )
    return value * half_up, slope


def body(
    nx, nh, ny,
    conv_hbm, grad_hbm, taps_hbm, win_ref, wout_ref, gate_hbm, slots_hbm, counts_hbm,
    out_ref, gin_ref, gout_ref,
    conv_ref, grad_ref, taps_ref, gate_ref, slots_ref, counts_ref, chosen,
    rows, w_in, w_out, part_to, part_from, relay, hidden, hidden_own, pre_grads, back_to, back_from,
    grads_own, grads_to, grads_from, field, rim, shifted,
    i_own, x_send, x_recv, w_own, w_send, w_recv, v_send, v_recv, u_send, u_recv,
    z_send, z_recv, p_send, p_recv, c_send, c_recv, e_send, e_recv,
    a_send, a_recv, b_send, b_recv, g_send, g_recv, h_send, h_recv,
):
    nz = nh // 2
    x, h, y = lax.axis_index("tm"), lax.axis_index("height"), lax.axis_index("expert")
    tokens, width = conv_ref.shape
    slot = slots_ref.shape[1]
    picks = nx * slot
    units = win_ref.shape[2]
    x_order, z_order = near_first(nx), near_first(nz)
    x_at = {d: i for i, d in enumerate(x_order)}
    z_at = {d: i for i, d in enumerate(z_order)}
    partner = h + 1 - 2 * lax.rem(h, 2)
    sides = [(a, b) for a in (-1, 0, 1) for b in (-1, 0, 1) if (a, b) != (0, 0)]
    steps = nz // 2
    spans = [(0, 3)] + [(2 * k - 1, 2 * k + 1) for k in range(2, steps)] + [(nz - 1, nz)]
    last_stage = len(spans) - 1
    relayed = last_stage - 1 if ny == 8 else 0

    def x_far(d):
        return lax.rem(x + d + nx, nx)

    def y_far(d):
        return lax.rem(y + d + ny, ny)

    def h_far(d):
        return lax.rem(h + d + nh, nh)

    def z_far(d):
        return lax.rem(h + 2 * d + nh, nh)

    def onward(way):
        return (x, z_far(-1 if way else 1), y)

    pending = []

    def remote(src, dst, sems_to, sems_from, device):
        copy = pltpu.make_async_remote_copy(
            src_ref=src, dst_ref=dst, send_sem=sems_to, recv_sem=sems_from,
            device_id=device, device_id_type=MESH,
        )
        copy.start()
        pending.append(copy)
        return copy

    peers = [(x_far(d), h, y) for d in range(1, nx)]
    peers += [(x, h, y_far(d)) for d in range(1, ny)]
    peers += [(x, z_far(d), y) for d in range(1, nz)]
    peers += [(x, partner, y)]
    peers += [(x_far(a), h_far(b), y) for a, b in sides if b != 0]
    barrier = pltpu.get_barrier_semaphore()
    for peer in peers:
        pl.semaphore_signal(barrier, inc=1, device_id=peer, device_id_type=MESH)

    own, other = pl.ds(0, units), pl.ds(units, units)
    inputs = [
        pltpu.make_async_copy(src, dst, i_own.at[at])
        for at, (src, dst) in enumerate(
            [
                (slots_hbm, slots_ref), (counts_hbm, counts_ref), (gate_hbm, gate_ref),
                (conv_hbm, conv_ref), (grad_hbm, grad_ref), (taps_hbm, taps_ref),
            ]
        )
    ]
    own_weights = [
        pltpu.make_async_copy(win_ref.at[x], w_in.at[0, :, own], w_own.at[0]),
        pltpu.make_async_copy(wout_ref.at[x], w_out.at[0, own], w_own.at[1]),
    ]
    for copy in inputs + own_weights:
        copy.start()

    lane = lax.broadcasted_iota(jnp.int32, (nx, picks), 1)
    expert_row = lax.broadcasted_iota(jnp.int32, (nx, picks), 0)
    mine = (lane // slot == expert_row).astype(FULL)
    spread_row = lax.broadcasted_iota(jnp.int32, (slot, picks), 0)
    spread_lane = lax.broadcasted_iota(jnp.int32, (slot, picks), 1)
    spread = (lax.rem(spread_lane, slot) == spread_row).astype(FULL)
    gate_row_at = lax.broadcasted_iota(jnp.int32, (nh * slot, picks), 0)
    gate_lane = lax.broadcasted_iota(jnp.int32, (nh * slot, picks), 1)
    gate_pick = (gate_row_at == h * slot + lax.rem(gate_lane, slot)).astype(FULL)
    token = lax.broadcasted_iota(jnp.int32, (tokens, picks), 0).astype(FULL)
    lane_row = lax.broadcasted_iota(jnp.int32, (1, picks), 1)
    for copy in inputs:
        copy.wait()
    index_row = jnp.sum(
        mine * dot_nn(slots_ref[...].astype(FULL), spread), axis=0, keepdims=True
    )
    count_row = dot_nn(counts_ref[...].astype(FULL), mine)
    live = lax.rem(lane_row, slot).astype(FULL) < count_row - 0.5
    index_row = jnp.where(live, index_row, -1.0)
    gate_row = jnp.sum(
        mine
        * lax.dot_general(
            gate_ref[...], gate_pick, (((1,), (0,)), ((), ())),
            precision=lax.Precision.HIGHEST, preferred_element_type=FULL,
        ),
        axis=0,
        keepdims=True,
    )
    selector = (token == index_row).astype(HALF)
    gates = jnp.transpose(jnp.broadcast_to(gate_row, (picks, picks)))
    gates = jnp.concatenate([gates] * (width // picks), axis=1)
    conv_rows = dot_tn(selector, conv_ref[...]).astype(HALF)
    grad_rows = (dot_tn(selector, grad_ref[...]) * gates).astype(HALF)
    chosen[:, 0] = conv_rows.reshape(nx, slot, width)
    chosen[:, 1] = grad_rows.reshape(nx, slot, width)
    rows[0, 0] = chosen[x]

    pl.semaphore_wait(barrier, len(peers))

    x_copies = {}
    for d in x_order[1:]:
        there = x_at[nx - d]
        x_copies[there] = remote(
            chosen.at[x_far(d)], rows.at[0, there], x_send.at[there], x_recv.at[there],
            (x_far(d), h, y),
        )
    weight_copies = [
        remote(win_ref.at[x], w_in.at[0, :, other], w_send.at[0], w_recv.at[0],
               (x, partner, y)),
        remote(wout_ref.at[x], w_out.at[0, other], w_send.at[1], w_recv.at[1],
               (x, partner, y)),
    ]

    v_copies, u_copies = {}, {}

    def v_block(step, way):
        return z_at[(step if way else nz - step) % nz]

    def v_half(block, part, half):
        return w_out.at[block, half] if part else w_in.at[block, :, half]

    def v_goes(step, part, way):
        return step < steps or (step == steps and part == way)

    def v_forward(step, part, way):
        key = ((step - 1) * 2 + part) * 2 + way
        if step == 1:
            source = (wout_ref if part else win_ref).at[x]
        else:
            source = v_half(v_block(step - 1, way), part, own)
        v_copies[step, part, way] = remote(
            source, v_half(v_block(step, way), part, own), v_send.at[key], v_recv.at[key],
            onward(way),
        )

    def v_arrive(step):
        for part in (0, 1):
            for way in (0, 1):
                if v_goes(step, part, way):
                    v_copies[step, part, way].wait_recv()
                    if step < steps and v_goes(step + 1, part, way):
                        v_forward(step + 1, part, way)
                    block, key = v_block(step, way), ((step - 1) * 2 + part) * 2 + way
                    u_copies[step, part, way] = remote(
                        v_half(block, part, own), v_half(block, part, other),
                        u_send.at[key], u_recv.at[key], (x, partner, y),
                    )

    parts = min(2, nx)
    split = nx // parts
    z_copies = {}

    def z_forward(step, part, way):
        source = (step - 1) if way == 1 else (nz - step + 1) % nz
        target = step if way == 1 else (nz - step) % nz
        key = ((step - 1) * parts + part) * 2 + way
        groups = pl.ds(part * split, split)
        z_copies[step, part, way] = remote(
            rows.at[z_at[source], groups], rows.at[z_at[target], groups],
            z_send.at[key], z_recv.at[key], onward(way),
        )

    def z_goes(step, part, way):
        return step < steps or (step == steps and (2 * part // parts) == way)

    def z_start():
        for part in range(parts):
            for way in (0, 1):
                if z_goes(1, part, way):
                    z_forward(1, part, way)

    def z_arrive(step):
        if step > steps:
            return
        for part in range(parts):
            for way in (0, 1):
                if z_goes(step, part, way):
                    z_copies[step, part, way].wait_recv()
                    if step < steps and z_goes(step + 1, part, way):
                        z_forward(step + 1, part, way)

    p_copies, c_copies, e_copies = {}, {}, {}

    def p_send_to(stage, at, source, target, distance):
        key = stage * ny + at
        p_copies[stage, at] = remote(
            source, target, p_send.at[key], p_recv.at[key], (x, h, y_far(distance)))

    def e_send_to(stage, at, piece, distance):
        key = stage * ny + at
        e_copies[stage, at] = remote(
            piece, piece, e_send.at[key], e_recv.at[key], (x, h, y_far(distance)))

    def cut(stage):
        first, last = spans[stage]
        middle = first + (last - first + 1) // 2
        return first, middle, last

    def partial_sums(stage):
        first, middle, last = cut(stage)
        for part in (0, 1):
            for way in (0, 1):
                for step in ([1] if stage == 0 else [stage + 1]):
                    if (step, part, way) in u_copies:
                        u_copies[step, part, way].wait_recv()
        conv_block = rows[0, :, 0].reshape(picks, width)
        grad_block = rows[0, :, 1].reshape(picks, width)
        for block in range(first, last):
            part_to[:, block, 0] = dot_nn(conv_block, w_in[block]).astype(HALF).reshape(
                ny, slot, 2 * units)
            part_to[:, block, 1] = dot_nt(grad_block, w_out[block]).astype(HALF).reshape(
                ny, slot, 2 * units)
        span = pl.ds(first, last - first)
        if stage >= relayed:
            for d in reversed(near_first(ny)[1:]):
                p_send_to(stage, ny - d, part_to.at[y_far(d), span],
                          part_from.at[ny - d, span], d)
            return
        for way in (1, -1):
            p_send_to(stage, 4 - way, part_to.at[y_far(-3 * way), span],
                      part_from.at[4 - way, span], -way)
        for way, lines in ((1, pl.ds(first, middle - first)), (-1, pl.ds(middle, last - middle))):
            p_send_to(stage, 4 if way == 1 else 0, part_to.at[y_far(4), lines],
                      part_from.at[4, lines], -2 * way)
        for way in (1, -1):
            p_send_to(stage, 4 - 3 * way, part_to.at[y_far(-way), span],
                      part_from.at[4 - 3 * way, span], -way)

    def relay_sums(stage):
        if stage >= relayed:
            return
        first, middle, last = cut(stage)
        span = pl.ds(first, last - first)
        for way, start, stop in ((1, first, middle), (-1, middle, last)):
            p_copies[stage, 4 - way].wait_recv()
            p_copies[stage, 4 if way == 1 else 0].wait_recv()
            lines = pl.ds(start, stop - start)
            relay[int(way > 0), span] = (
                part_to[y_far(-2 * way), span].astype(FULL)
                + part_from[4 - way, span].astype(FULL)
            ).astype(HALF)
            relay[int(way > 0), lines] = (
                part_to[y_far(-2 * way), lines].astype(FULL)
                + part_from[4 - way, lines].astype(FULL)
                + part_from[4, lines].astype(FULL)
            ).astype(HALF)
            p_send_to(stage, 4 - 2 * way, relay.at[int(way > 0), span],
                      part_from.at[4 - 2 * way, span], -2 * way)

    def own_hidden(stage):
        first, middle, last = cut(stage)
        span = pl.ds(first, last - first)
        total = part_to[y, span].astype(FULL)
        for d in ((1, 7, 2, 6) if stage < relayed else range(1, ny)):
            p_copies[stage, d].wait_recv()
            total = total + part_from[d, span].astype(FULL)
        activated, slope = gelu_and_slope(total[:, 0])
        grad_pre = (slope * total[:, 1]).astype(HALF)
        pre_grads[span, y] = grad_pre
        piece = pre_grads.at[span, y]
        if stage < relayed:
            for d in (2, 6, 1, 7):
                e_send_to(stage, ny - d, piece, d)
        else:
            for d in reversed(near_first(ny)[1:]):
                e_send_to(stage, ny - d, piece, d)
        hidden_own[span, 0] = activated.astype(HALF)
        hidden_own[span, 1] = grad_pre
        for block in range(first, last):
            distance = z_order[block]
            if distance == 0:
                hidden[0, y] = hidden_own[0]
                continue
            there = z_at[nz - distance]
            c_copies[there] = remote(
                hidden_own.at[block], hidden.at[there, y], c_send.at[there], c_recv.at[there],
                (x, z_far(distance), y),
            )

    def relay_grads(stage):
        if stage >= relayed:
            return
        first, middle, last = cut(stage)
        span = pl.ds(first, last - first)
        for way, lines in ((1, pl.ds(first, middle - first)), (-1, pl.ds(middle, last - middle))):
            e_copies[stage, 4 + 2 * way].wait_recv()
            source = y_far(-2 * way)
            e_send_to(stage, 4 + way, pre_grads.at[span, source], way)
            e_send_to(stage, 4 if way == 1 else 0, pre_grads.at[lines, source], 2 * way)

    for part in (0, 1):
        for way in (0, 1):
            if v_goes(1, part, way):
                v_forward(1, part, way)
    v_arrive(1)
    for copy in x_copies.values():
        copy.wait_recv()
    for copy in own_weights:
        copy.wait()
    for copy in weight_copies:
        copy.wait_recv()
    partial_sums(0)
    for stage in range(1, last_stage + 1):
        v_arrive(stage + 1)
        if stage == max(last_stage - 1, 1):
            z_start()
        partial_sums(stage)
        relay_sums(stage - 1)
        if stage >= 2:
            own_hidden(stage - 2)
    if last_stage >= 1:
        own_hidden(last_stage - 1)

    y_steps = ny // 2
    bound = spans[max(last_stage - 2, 0)][1]
    blocks = (pl.ds(0, bound), pl.ds(bound, nz - bound))
    a_copies = {}

    def a_forward(step, part, way):
        piece = y_far(step - 1) if way == 1 else y_far(1 - step)
        key = ((step - 1) * 2 + part) * 2 + way
        a_copies[step, part, way] = remote(
            hidden.at[blocks[part], piece], hidden.at[blocks[part], piece],
            a_send.at[key], a_recv.at[key], (x, h, y_far(-1) if way == 1 else y_far(1)),
        )

    def a_goes(step, part, way):
        return step < y_steps or (step == y_steps and part == way)

    def a_start(part):
        for block in range(nz):
            if (block < bound) == (part == 0) and block in c_copies:
                c_copies[block].wait_recv()
        for way in (0, 1):
            if a_goes(1, part, way):
                a_forward(1, part, way)

    def a_arrive(step, part):
        if step > y_steps:
            return
        for way in (0, 1):
            if a_goes(step, part, way):
                a_copies[step, part, way].wait_recv()
                if step < y_steps and a_goes(step + 1, part, way):
                    a_forward(step + 1, part, way)

    for stage in range(last_stage - 1):
        relay_grads(stage)
    z_arrive(1)
    a_start(0)
    own_hidden(last_stage)
    z_arrive(2)
    a_start(1)
    a_arrive(1, 0)

    total = jnp.zeros((picks, width), FULL)
    for stage in range(last_stage + 1):
        for d in range(ny):
            if (stage, d) in e_copies and not (stage < relayed and d in (2, 6)):
                e_copies[stage, d].wait_recv()
        for block in range(*spans[stage]):
            total += dot_nt(pre_grads[block].reshape(picks, 2 * units), w_in[block])
    back_to[...] = total.astype(HALF).reshape(nx, slot, width)

    b_copies = []
    for d in x_order[1:]:
        b_copies.append(
            remote(back_to.at[x_at[d]], back_from.at[x], b_send.at[d], b_recv.at[d],
                   (x_far(d), h, y))
        )
    back_from[x] = back_to[0]
    a_arrive(1, 1)
    a_arrive(2, 0)
    z_arrive(3)
    for copy in b_copies:
        copy.wait_recv()
    added = dot_nn(selector, back_from[...].reshape(picks, width))
    total_field = grad_ref[...].astype(FULL) + added
    frames, grid_rows, columns, _ = out_ref.shape
    rim[pl.ds(1, frames), pl.ds(1, grid_rows)] = total_field.astype(HALF).reshape(
        frames, grid_rows, columns, width)

    def face(side, size, inside):
        if side == 0:
            return pl.ds(1, size)
        if inside:
            return pl.ds(1 if side < 0 else size, 1)
        return pl.ds(size + 1 if side < 0 else 0, 1)

    h_copies = []
    for at, (a, b) in enumerate(sides):
        h_copies.append(
            remote(
                rim.at[face(a, frames, True), face(b, grid_rows, True)],
                rim.at[face(a, frames, False), face(b, grid_rows, False)],
                h_send.at[at], h_recv.at[at], (x_far(a), h_far(b), y),
            )
        )
    field[...] = total_field.reshape(frames, grid_rows, columns, width)
    a_arrive(2, 1)
    a_arrive(3, 0)

    at_column = lax.broadcasted_iota(jnp.int32, (columns, width), 0)

    def shift_cell(f, r, here):
        shifted[1, f, r] = here
        shifted[0, f, r] = jnp.where(
            at_column == columns - 1, 0.0, pltpu.roll(here, columns - 1, 0))
        shifted[2, f, r] = jnp.where(at_column == 0, 0.0, pltpu.roll(here, 1, 0))

    def shift_inner(cell, _):
        f, r = 1 + cell // grid_rows, 1 + lax.rem(cell, grid_rows)
        shift_cell(f, r, rim[f, r].astype(FULL))
        return _

    lax.fori_loop(0, frames * grid_rows, shift_inner, 0)
    a_arrive(3, 1)
    for copy in h_copies:
        copy.wait_recv()

    def shift_outer(cell, f, r):
        outside = ((f == 0) & (x == 0)) | ((f == frames + 1) & (x == nx - 1))
        outside |= ((r == 0) & (h == 0)) | ((r == grid_rows + 1) & (h == nh - 1))
        shift_cell(f, r, jnp.where(outside, 0.0, rim[f, r].astype(FULL)))
        return cell

    def shift_ends(cell, _):
        return shift_outer(
            _, (cell // (grid_rows + 2)) * (frames + 1), lax.rem(cell, grid_rows + 2))

    def shift_sides(cell, _):
        return shift_outer(_, 1 + cell // 2, lax.rem(cell, 2) * (grid_rows + 1))

    lax.fori_loop(0, 2 * (grid_rows + 2), shift_ends, 0)
    lax.fori_loop(0, 2 * frames, shift_sides, 0)

    def convolve(f, _):
        total = field[f]
        for a in range(3):
            for b in range(3):
                for k in range(3):
                    tap = taps_ref[pl.ds(9 * a + 3 * b + k, 1)].reshape(1, 1, width)
                    total = total + tap * shifted[k, f + 2 - a, pl.ds(2 - b, grid_rows)]
        out_ref[f] = total
        return _

    lax.fori_loop(0, frames, convolve, 0)

    for step in range(4, steps + 1):
        z_arrive(step)
    for step in range(4, y_steps + 1):
        for part in (0, 1):
            a_arrive(step, part)
    activated = hidden[:, :, 0].reshape(nz * picks, 2 * units)
    grads = dot_tn(activated, rows[:, :, 1].reshape(nz * picks, width))
    gout_ref[...] = grads[:units]
    grads_to[0] = grads[units:]
    g_copies = [remote(grads_to.at[0], grads_from.at[0], g_send.at[0], g_recv.at[0],
                       (x, partner, y))]
    grad_pre = hidden[:, :, 1].reshape(nz * picks, 2 * units)
    grads = dot_tn(grad_pre, rows[:, :, 0].reshape(nz * picks, width))
    grads_own[...] = grads[:units]
    grads_to[1] = grads[units:]
    g_copies.append(remote(grads_to.at[1], grads_from.at[1], g_send.at[1], g_recv.at[1],
                           (x, partner, y)))
    g_copies[0].wait_recv()
    gout_ref[...] += grads_from[0]
    g_copies[1].wait_recv()
    gin_ref[...] = jnp.transpose(grads_own[...] + grads_from[1])

    for copy in pending:
        copy.wait_send()


def on_device(
    nx, nh, ny,
    saved_conv, grad_out, conv_kernel, weight_in, weight_out, gate_values, picked_slots, slot_counts,
):
    nz = nh // 2
    frames, grid_rows, columns, width = saved_conv.shape
    tokens = frames * grid_rows * columns
    experts, _, units = weight_in.shape
    slot = picked_slots.shape[3]
    picks = experts * slot
    vmem = pl.BlockSpec(memory_space=pltpu.VMEM)
    hbm = pl.BlockSpec(memory_space=pltpu.HBM)
    steps = nz // 2
    dma = pltpu.SemaphoreType.DMA
    out, grad_in, grad_w = pl.pallas_call(
        functools.partial(body, nx, nh, ny),
        out_shape=(
            jax.ShapeDtypeStruct((frames, grid_rows, columns, width), FULL),
            jax.ShapeDtypeStruct((width, units), FULL),
            jax.ShapeDtypeStruct((units, width), FULL),
        ),
        in_specs=[hbm] * 8,
        out_specs=(vmem, vmem, vmem),
        scratch_shapes=[
            pltpu.VMEM((tokens, width), HALF),
            pltpu.VMEM((tokens, width), HALF),
            pltpu.VMEM(conv_kernel.shape, FULL),
            pltpu.VMEM(gate_values.shape[1:], FULL),
            pltpu.VMEM((experts, slot), jnp.int32),
            pltpu.VMEM((1, experts), jnp.int32),
            pltpu.VMEM((experts, 2, slot, width), HALF),
            pltpu.VMEM((nz, nx, 2, slot, width), HALF),
            pltpu.VMEM((nz, width, 2 * units), HALF),
            pltpu.VMEM((nz, 2 * units, width), HALF),
            pltpu.VMEM((ny, nz, 2, slot, 2 * units), HALF),
            pltpu.VMEM((ny, nz, 2, slot, 2 * units), HALF),
            pltpu.VMEM((2, nz, 2, slot, 2 * units), HALF),
            pltpu.VMEM((nz, ny, 2, slot, 2 * units), HALF),
            pltpu.VMEM((nz, 2, slot, 2 * units), HALF),
            pltpu.VMEM((nz, ny, slot, 2 * units), HALF),
            pltpu.VMEM((nx, slot, width), HALF),
            pltpu.VMEM((nx, slot, width), HALF),
            pltpu.VMEM((units, width), FULL),
            pltpu.VMEM((2, units, width), FULL),
            pltpu.VMEM((2, units, width), FULL),
            pltpu.VMEM((frames, grid_rows, columns, width), FULL),
            pltpu.VMEM((frames + 2, grid_rows + 2, columns, width), HALF),
            pltpu.VMEM((3, frames + 2, grid_rows + 2, columns, width), FULL),
            dma((6,)), dma((nx,)), dma((nx,)),
            dma((2,)), dma((2,)), dma((2,)),
            dma((4 * steps,)), dma((4 * steps,)), dma((4 * steps,)), dma((4 * steps,)),
            dma((8 * steps,)), dma((8 * steps,)),
            dma(((steps + 1) * ny,)), dma(((steps + 1) * ny,)),
            dma((nz,)), dma((nz,)),
            dma(((steps + 1) * ny,)), dma(((steps + 1) * ny,)),
            dma((2 * ny,)), dma((2 * ny,)),
            dma((nx,)), dma((nx,)),
            dma((2,)), dma((2,)),
            dma((8,)), dma((8,)),
        ],
        compiler_params=pltpu.CompilerParams(
            collective_id=0, has_side_effects=True, vmem_limit_bytes=62 * 1024 * 1024
        ),
    )(
        saved_conv.reshape(tokens, width),
        grad_out.reshape(tokens, width),
        conv_kernel,
        weight_in,
        weight_out,
        gate_values.reshape(gate_values.shape[1:]),
        picked_slots.reshape(experts, slot),
        slot_counts.reshape(1, experts),
    )
    return out, grad_in[None], grad_w[None]


def solution(mesh):
    placed = (
        P("tm", "height", None, "expert"),
        P("tm", "height", None, "expert"),
        P(None, "expert"),
        P(None, "expert", "height"),
        P(None, "height", "expert"),
        P("tm", None, None),
        P("tm", "height", None, None),
        P("tm", "height", None),
    )
    sizes = (mesh.shape["tm"], mesh.shape["height"], mesh.shape["expert"])
    return jax.shard_map(
        functools.partial(on_device, *sizes),
        mesh=mesh,
        in_specs=placed,
        out_specs=(
            P("tm", "height", None, "expert"),
            P("tm", "expert", "height"),
            P("tm", "height", "expert"),
        ),
        check_vma=False,
    )
```

```python
import functools

import jax
import jax.numpy as jnp
from jax import lax
from jax.experimental import pallas as pl
from jax.experimental.pallas import tpu as pltpu
from jax.sharding import PartitionSpec as P

MESH = pl.DeviceIdType.MESH
HALF = jnp.bfloat16
FULL = jnp.float32


def near_first(count):
    order = [0]
    for step in range(1, count // 2):
        order += [step, count - step]
    return order + [count // 2]


def dot_nn(a, b):
    return lax.dot_general(a, b, (((1,), (0,)), ((), ())), preferred_element_type=FULL)


def dot_nt(a, b):
    return lax.dot_general(a, b, (((1,), (1,)), ((), ())), preferred_element_type=FULL)


def dot_tn(a, b):
    return lax.dot_general(a, b, (((0,), (0,)), ((), ())), preferred_element_type=FULL)


def gelu_and_slope(value):
    scale = 0.7978845608028654
    square = value * value
    tanh = jnp.tanh(scale * (value + 0.044715 * value * square))
    half_up = 0.5 * (1.0 + tanh)
    slope = half_up + 0.5 * value * (1.0 - tanh * tanh) * (
        scale * (1.0 + 3.0 * 0.044715 * square)
    )
    return value * half_up, slope


def body(
    nx, nh, ny,
    conv_hbm, grad_hbm, taps_hbm, win_ref, wout_ref, gate_hbm, slots_hbm, counts_hbm,
    out_ref, gin_ref, gout_ref,
    conv_ref, grad_ref, taps_ref, gate_ref, slots_ref, counts_ref, chosen,
    rows, w_in, w_out, part_to, part_from, relay, hidden, hidden_own, pre_grads, back_to, back_from,
    grads_own, grads_to, grads_from, field, rim, shifted,
    i_own, x_send, x_recv, w_own, w_send, w_recv, v_send, v_recv, u_send, u_recv,
    z_send, z_recv, p_send, p_recv, c_send, c_recv, e_send, e_recv,
    a_send, a_recv, b_send, b_recv, g_send, g_recv, h_send, h_recv,
):
    nz = nh // 2
    x, h, y = lax.axis_index("tm"), lax.axis_index("height"), lax.axis_index("expert")
    tokens, width = conv_ref.shape
    slot = slots_ref.shape[1]
    picks = nx * slot
    units = win_ref.shape[2]
    x_order, z_order = near_first(nx), near_first(nz)
    x_at = {d: i for i, d in enumerate(x_order)}
    z_at = {d: i for i, d in enumerate(z_order)}
    partner = h + 1 - 2 * lax.rem(h, 2)
    sides = [(a, b) for a in (-1, 0, 1) for b in (-1, 0, 1) if (a, b) != (0, 0)]
    steps = nz // 2
    spans = [(0, 3)] + [(2 * k - 1, 2 * k + 1) for k in range(2, steps)] + [(nz - 1, nz)]
    last_stage = len(spans) - 1
    relayed = last_stage - 1 if ny == 8 else 0

    def x_far(d):
        return lax.rem(x + d + nx, nx)

    def y_far(d):
        return lax.rem(y + d + ny, ny)

    def h_far(d):
        return lax.rem(h + d + nh, nh)

    def z_far(d):
        return lax.rem(h + 2 * d + nh, nh)

    def onward(way):
        return (x, z_far(-1 if way else 1), y)

    pending = []

    def remote(src, dst, sems_to, sems_from, device):
        copy = pltpu.make_async_remote_copy(
            src_ref=src, dst_ref=dst, send_sem=sems_to, recv_sem=sems_from,
            device_id=device, device_id_type=MESH,
        )
        copy.start()
        pending.append(copy)
        return copy

    peers = [(x_far(d), h, y) for d in range(1, nx)]
    peers += [(x, h, y_far(d)) for d in range(1, ny)]
    peers += [(x, z_far(d), y) for d in range(1, nz)]
    peers += [(x, partner, y)]
    peers += [(x_far(a), h_far(b), y) for a, b in sides if b != 0]
    barrier = pltpu.get_barrier_semaphore()
    for peer in peers:
        pl.semaphore_signal(barrier, inc=1, device_id=peer, device_id_type=MESH)

    own, other = pl.ds(0, units), pl.ds(units, units)
    inputs = [
        pltpu.make_async_copy(src, dst, i_own.at[at])
        for at, (src, dst) in enumerate(
            [
                (slots_hbm, slots_ref), (counts_hbm, counts_ref), (gate_hbm, gate_ref),
                (conv_hbm, conv_ref), (grad_hbm, grad_ref), (taps_hbm, taps_ref),
            ]
        )
    ]
    own_weights = [
        pltpu.make_async_copy(win_ref.at[x], w_in.at[0, :, own], w_own.at[0]),
        pltpu.make_async_copy(wout_ref.at[x], w_out.at[0, own], w_own.at[1]),
    ]
    for copy in inputs + own_weights:
        copy.start()

    pl.semaphore_wait(barrier, len(peers))

    weight_copies = [
        remote(win_ref.at[x], w_in.at[0, :, other], w_send.at[0], w_recv.at[0],
               (x, partner, y)),
        remote(wout_ref.at[x], w_out.at[0, other], w_send.at[1], w_recv.at[1],
               (x, partner, y)),
    ]

    v_copies, u_copies = {}, {}

    def v_block(step, way):
        return z_at[(step if way else nz - step) % nz]

    def v_half(block, part, half):
        return w_out.at[block, half] if part else w_in.at[block, :, half]

    def v_goes(step, part, way):
        return step < steps or (step == steps and part == way)

    def v_forward(step, part, way):
        key = ((step - 1) * 2 + part) * 2 + way
        if step == 1:
            source = (wout_ref if part else win_ref).at[x]
        else:
            source = v_half(v_block(step - 1, way), part, own)
        v_copies[step, part, way] = remote(
            source, v_half(v_block(step, way), part, own), v_send.at[key], v_recv.at[key],
            onward(way),
        )

    def v_arrive(step):
        for part in (0, 1):
            for way in (0, 1):
                if v_goes(step, part, way):
                    v_copies[step, part, way].wait_recv()
                    if step < steps and v_goes(step + 1, part, way):
                        v_forward(step + 1, part, way)
                    block, key = v_block(step, way), ((step - 1) * 2 + part) * 2 + way
                    u_copies[step, part, way] = remote(
                        v_half(block, part, own), v_half(block, part, other),
                        u_send.at[key], u_recv.at[key], (x, partner, y),
                    )

    for way in (0, 1):
        if v_goes(1, 0, way):
            v_forward(1, 0, way)

    lane = lax.broadcasted_iota(jnp.int32, (nx, picks), 1)
    expert_row = lax.broadcasted_iota(jnp.int32, (nx, picks), 0)
    mine = (lane // slot == expert_row).astype(FULL)
    spread_row = lax.broadcasted_iota(jnp.int32, (slot, picks), 0)
    spread_lane = lax.broadcasted_iota(jnp.int32, (slot, picks), 1)
    spread = (lax.rem(spread_lane, slot) == spread_row).astype(FULL)
    gate_row_at = lax.broadcasted_iota(jnp.int32, (nh * slot, picks), 0)
    gate_lane = lax.broadcasted_iota(jnp.int32, (nh * slot, picks), 1)
    gate_pick = (gate_row_at == h * slot + lax.rem(gate_lane, slot)).astype(FULL)
    token = lax.broadcasted_iota(jnp.int32, (tokens, picks), 0).astype(FULL)
    lane_row = lax.broadcasted_iota(jnp.int32, (1, picks), 1)
    for copy in inputs:
        copy.wait()
    index_row = jnp.sum(
        mine * dot_nn(slots_ref[...].astype(FULL), spread), axis=0, keepdims=True
    )
    count_row = dot_nn(counts_ref[...].astype(FULL), mine)
    live = lax.rem(lane_row, slot).astype(FULL) < count_row - 0.5
    index_row = jnp.where(live, index_row, -1.0)
    gate_row = jnp.sum(
        mine
        * lax.dot_general(
            gate_ref[...], gate_pick, (((1,), (0,)), ((), ())),
            precision=lax.Precision.HIGHEST, preferred_element_type=FULL,
        ),
        axis=0,
        keepdims=True,
    )
    selector = (token == index_row).astype(HALF)
    gates = jnp.transpose(jnp.broadcast_to(gate_row, (picks, picks)))
    gates = jnp.concatenate([gates] * (width // picks), axis=1)
    conv_rows = dot_tn(selector, conv_ref[...]).astype(HALF)
    grad_rows = (dot_tn(selector, grad_ref[...]) * gates).astype(HALF)
    chosen[:, 0] = conv_rows.reshape(nx, slot, width)
    chosen[:, 1] = grad_rows.reshape(nx, slot, width)
    rows[0, 0] = chosen[x]

    x_copies = {}
    for d in x_order[1:]:
        there = x_at[nx - d]
        x_copies[there] = remote(
            chosen.at[x_far(d)], rows.at[0, there], x_send.at[there], x_recv.at[there],
            (x_far(d), h, y),
        )
    parts = min(2, nx)
    split = nx // parts
    z_copies = {}

    def z_forward(step, part, way):
        source = (step - 1) if way == 1 else (nz - step + 1) % nz
        target = step if way == 1 else (nz - step) % nz
        key = ((step - 1) * parts + part) * 2 + way
        groups = pl.ds(part * split, split)
        z_copies[step, part, way] = remote(
            rows.at[z_at[source], groups], rows.at[z_at[target], groups],
            z_send.at[key], z_recv.at[key], onward(way),
        )

    def z_goes(step, part, way):
        return step < steps or (step == steps and (2 * part // parts) == way)

    def z_start(part):
        for way in (0, 1):
            if z_goes(1, part, way):
                z_forward(1, part, way)

    def z_arrive(step):
        if step > steps:
            return
        for part in range(parts):
            for way in (0, 1):
                if z_goes(step, part, way):
                    z_copies[step, part, way].wait_recv()
                    if step < steps and z_goes(step + 1, part, way):
                        z_forward(step + 1, part, way)

    p_copies, c_copies, e_copies = {}, {}, {}

    def p_send_to(stage, at, source, target, distance):
        key = stage * ny + at
        p_copies[stage, at] = remote(
            source, target, p_send.at[key], p_recv.at[key], (x, h, y_far(distance)))

    def e_send_to(stage, at, piece, distance):
        key = stage * ny + at
        e_copies[stage, at] = remote(
            piece, piece, e_send.at[key], e_recv.at[key], (x, h, y_far(distance)))

    def cut(stage):
        first, last = spans[stage]
        middle = first + (last - first + 1) // 2
        return first, middle, last

    def partial_sums(stage):
        first, middle, last = cut(stage)
        for part in (0, 1):
            for way in (0, 1):
                for step in ([1] if stage == 0 else [stage + 1]):
                    if (step, part, way) in u_copies:
                        u_copies[step, part, way].wait_recv()
        conv_block = rows[0, :, 0].reshape(picks, width)
        grad_block = rows[0, :, 1].reshape(picks, width)
        for block in range(first, last):
            part_to[:, block, 0] = dot_nn(conv_block, w_in[block]).astype(HALF).reshape(
                ny, slot, 2 * units)
            part_to[:, block, 1] = dot_nt(grad_block, w_out[block]).astype(HALF).reshape(
                ny, slot, 2 * units)
        span = pl.ds(first, last - first)
        if stage >= relayed:
            for d in reversed(near_first(ny)[1:]):
                p_send_to(stage, ny - d, part_to.at[y_far(d), span],
                          part_from.at[ny - d, span], d)
            return
        for way in (1, -1):
            p_send_to(stage, 4 - way, part_to.at[y_far(-3 * way), span],
                      part_from.at[4 - way, span], -way)
        for way, lines in ((1, pl.ds(first, middle - first)), (-1, pl.ds(middle, last - middle))):
            p_send_to(stage, 4 if way == 1 else 0, part_to.at[y_far(4), lines],
                      part_from.at[4, lines], -2 * way)
        for way in (1, -1):
            p_send_to(stage, 4 - 3 * way, part_to.at[y_far(-way), span],
                      part_from.at[4 - 3 * way, span], -way)

    def relay_sums(stage):
        if stage >= relayed:
            return
        first, middle, last = cut(stage)
        span = pl.ds(first, last - first)
        for way, start, stop in ((1, first, middle), (-1, middle, last)):
            p_copies[stage, 4 - way].wait_recv()
            p_copies[stage, 4 if way == 1 else 0].wait_recv()
            lines = pl.ds(start, stop - start)
            relay[int(way > 0), span] = (
                part_to[y_far(-2 * way), span].astype(FULL)
                + part_from[4 - way, span].astype(FULL)
            ).astype(HALF)
            relay[int(way > 0), lines] = (
                part_to[y_far(-2 * way), lines].astype(FULL)
                + part_from[4 - way, lines].astype(FULL)
                + part_from[4, lines].astype(FULL)
            ).astype(HALF)
            p_send_to(stage, 4 - 2 * way, relay.at[int(way > 0), span],
                      part_from.at[4 - 2 * way, span], -2 * way)

    def own_hidden(stage):
        first, middle, last = cut(stage)
        span = pl.ds(first, last - first)
        total = part_to[y, span].astype(FULL)
        for d in ((1, 7, 2, 6) if stage < relayed else range(1, ny)):
            p_copies[stage, d].wait_recv()
            total = total + part_from[d, span].astype(FULL)
        activated, slope = gelu_and_slope(total[:, 0])
        grad_pre = (slope * total[:, 1]).astype(HALF)
        pre_grads[span, y] = grad_pre
        piece = pre_grads.at[span, y]
        if stage < relayed:
            for d in (2, 6, 1, 7):
                e_send_to(stage, ny - d, piece, d)
        else:
            for d in reversed(near_first(ny)[1:]):
                e_send_to(stage, ny - d, piece, d)
        hidden_own[span, 0] = activated.astype(HALF)
        hidden_own[span, 1] = grad_pre
        for block in range(first, last):
            distance = z_order[block]
            if distance == 0:
                hidden[0, y] = hidden_own[0]
                continue
            there = z_at[nz - distance]
            c_copies[there] = remote(
                hidden_own.at[block], hidden.at[there, y], c_send.at[there], c_recv.at[there],
                (x, z_far(distance), y),
            )

    def relay_grads(stage):
        if stage >= relayed:
            return
        first, middle, last = cut(stage)
        span = pl.ds(first, last - first)
        for way, lines in ((1, pl.ds(first, middle - first)), (-1, pl.ds(middle, last - middle))):
            e_copies[stage, 4 + 2 * way].wait_recv()
            source = y_far(-2 * way)
            e_send_to(stage, 4 + way, pre_grads.at[span, source], way)
            e_send_to(stage, 4 if way == 1 else 0, pre_grads.at[lines, source], 2 * way)

    for copy in own_weights:
        copy.wait()
    for copy in weight_copies:
        copy.wait_recv()
    for way in (0, 1):
        if v_goes(1, 1, way):
            v_forward(1, 1, way)
    v_arrive(1)
    for copy in x_copies.values():
        copy.wait_recv()
    partial_sums(0)
    for stage in range(1, last_stage + 1):
        v_arrive(stage + 1)
        if stage == max(last_stage - 1, 1):
            for part in range(parts):
                z_start(part)
        partial_sums(stage)
        relay_sums(stage - 1)
        if stage >= 2:
            own_hidden(stage - 2)
    if last_stage >= 1:
        own_hidden(last_stage - 1)
    z_arrive(1)

    y_steps = ny // 2
    bound = spans[max(last_stage - 2, 0)][1]
    blocks = (pl.ds(0, bound), pl.ds(bound, nz - bound))
    a_copies = {}

    def a_forward(step, part, way):
        piece = y_far(step - 1) if way == 1 else y_far(1 - step)
        key = ((step - 1) * 2 + part) * 2 + way
        a_copies[step, part, way] = remote(
            hidden.at[blocks[part], piece], hidden.at[blocks[part], piece],
            a_send.at[key], a_recv.at[key], (x, h, y_far(-1) if way == 1 else y_far(1)),
        )

    def a_goes(step, part, way):
        return step < y_steps or (step == y_steps and part == way)

    def a_start(part):
        for block in range(nz):
            if (block < bound) == (part == 0) and block in c_copies:
                c_copies[block].wait_recv()
        for way in (0, 1):
            if a_goes(1, part, way):
                a_forward(1, part, way)

    def a_arrive(step, part):
        if step > y_steps:
            return
        for way in (0, 1):
            if a_goes(step, part, way):
                a_copies[step, part, way].wait_recv()
                if step < y_steps and a_goes(step + 1, part, way):
                    a_forward(step + 1, part, way)

    for stage in range(last_stage):
        relay_grads(stage)
    own_hidden(last_stage)
    a_start(0)
    z_arrive(2)
    a_start(1)
    a_arrive(1, 0)

    total = jnp.zeros((picks, width), FULL)
    for stage in range(last_stage + 1):
        for d in range(ny):
            if (stage, d) in e_copies and not (stage < relayed and d in (2, 6)):
                e_copies[stage, d].wait_recv()
        for block in range(*spans[stage]):
            total += dot_nt(pre_grads[block].reshape(picks, 2 * units), w_in[block])
    back_to[...] = total.astype(HALF).reshape(nx, slot, width)

    b_copies = []
    for d in x_order[1:]:
        b_copies.append(
            remote(back_to.at[x_at[d]], back_from.at[x], b_send.at[d], b_recv.at[d],
                   (x_far(d), h, y))
        )
    back_from[x] = back_to[0]
    a_arrive(1, 1)
    a_arrive(2, 0)
    z_arrive(3)
    for copy in b_copies:
        copy.wait_recv()
    added = dot_nn(selector, back_from[...].reshape(picks, width))
    total_field = grad_ref[...].astype(FULL) + added
    frames, grid_rows, columns, _ = out_ref.shape
    rim[pl.ds(1, frames), pl.ds(1, grid_rows)] = total_field.astype(HALF).reshape(
        frames, grid_rows, columns, width)

    def face(side, size, inside):
        if side == 0:
            return pl.ds(1, size)
        if inside:
            return pl.ds(1 if side < 0 else size, 1)
        return pl.ds(size + 1 if side < 0 else 0, 1)

    h_copies = []
    for at, (a, b) in enumerate(sides):
        h_copies.append(
            remote(
                rim.at[face(a, frames, True), face(b, grid_rows, True)],
                rim.at[face(a, frames, False), face(b, grid_rows, False)],
                h_send.at[at], h_recv.at[at], (x_far(a), h_far(b), y),
            )
        )
    field[...] = total_field.reshape(frames, grid_rows, columns, width)
    a_arrive(2, 1)
    a_arrive(3, 0)

    at_column = lax.broadcasted_iota(jnp.int32, (columns, width), 0)

    def shift_cell(f, r, here):
        shifted[1, f, r] = here
        shifted[0, f, r] = jnp.where(
            at_column == columns - 1, 0.0, pltpu.roll(here, columns - 1, 0))
        shifted[2, f, r] = jnp.where(at_column == 0, 0.0, pltpu.roll(here, 1, 0))

    def shift_inner(cell, _):
        f, r = 1 + cell // grid_rows, 1 + lax.rem(cell, grid_rows)
        shift_cell(f, r, rim[f, r].astype(FULL))
        return _

    lax.fori_loop(0, frames * grid_rows, shift_inner, 0)
    a_arrive(3, 1)
    for copy in h_copies:
        copy.wait_recv()

    def shift_outer(cell, f, r):
        outside = ((f == 0) & (x == 0)) | ((f == frames + 1) & (x == nx - 1))
        outside |= ((r == 0) & (h == 0)) | ((r == grid_rows + 1) & (h == nh - 1))
        shift_cell(f, r, jnp.where(outside, 0.0, rim[f, r].astype(FULL)))
        return cell

    def shift_ends(cell, _):
        return shift_outer(
            _, (cell // (grid_rows + 2)) * (frames + 1), lax.rem(cell, grid_rows + 2))

    def shift_sides(cell, _):
        return shift_outer(_, 1 + cell // 2, lax.rem(cell, 2) * (grid_rows + 1))

    lax.fori_loop(0, 2 * (grid_rows + 2), shift_ends, 0)
    lax.fori_loop(0, 2 * frames, shift_sides, 0)

    def convolve(f, _):
        total = field[f]
        for a in range(3):
            for b in range(3):
                for k in range(3):
                    tap = taps_ref[pl.ds(9 * a + 3 * b + k, 1)].reshape(1, 1, width)
                    total = total + tap * shifted[k, f + 2 - a, pl.ds(2 - b, grid_rows)]
        out_ref[f] = total
        return _

    lax.fori_loop(0, frames, convolve, 0)

    for step in range(4, steps + 1):
        z_arrive(step)
    for step in range(4, y_steps + 1):
        for part in (0, 1):
            a_arrive(step, part)
    activated = hidden[:, :, 0].reshape(nz * picks, 2 * units)
    grads = dot_tn(activated, rows[:, :, 1].reshape(nz * picks, width))
    gout_ref[...] = grads[:units]
    grads_to[0] = grads[units:]
    g_copies = [remote(grads_to.at[0], grads_from.at[0], g_send.at[0], g_recv.at[0],
                       (x, partner, y))]
    grad_pre = hidden[:, :, 1].reshape(nz * picks, 2 * units)
    grads = dot_tn(grad_pre, rows[:, :, 0].reshape(nz * picks, width))
    grads_own[...] = grads[:units]
    grads_to[1] = grads[units:]
    g_copies.append(remote(grads_to.at[1], grads_from.at[1], g_send.at[1], g_recv.at[1],
                           (x, partner, y)))
    g_copies[0].wait_recv()
    gout_ref[...] += grads_from[0]
    g_copies[1].wait_recv()
    gin_ref[...] = jnp.transpose(grads_own[...] + grads_from[1])

    for copy in pending:
        copy.wait_send()


def on_device(
    nx, nh, ny,
    saved_conv, grad_out, conv_kernel, weight_in, weight_out, gate_values, picked_slots, slot_counts,
):
    nz = nh // 2
    frames, grid_rows, columns, width = saved_conv.shape
    tokens = frames * grid_rows * columns
    experts, _, units = weight_in.shape
    slot = picked_slots.shape[3]
    picks = experts * slot
    vmem = pl.BlockSpec(memory_space=pltpu.VMEM)
    hbm = pl.BlockSpec(memory_space=pltpu.HBM)
    steps = nz // 2
    dma = pltpu.SemaphoreType.DMA
    out, grad_in, grad_w = pl.pallas_call(
        functools.partial(body, nx, nh, ny),
        out_shape=(
            jax.ShapeDtypeStruct((frames, grid_rows, columns, width), FULL),
            jax.ShapeDtypeStruct((width, units), FULL),
            jax.ShapeDtypeStruct((units, width), FULL),
        ),
        in_specs=[hbm] * 8,
        out_specs=(vmem, vmem, vmem),
        scratch_shapes=[
            pltpu.VMEM((tokens, width), HALF),
            pltpu.VMEM((tokens, width), HALF),
            pltpu.VMEM(conv_kernel.shape, FULL),
            pltpu.VMEM(gate_values.shape[1:], FULL),
            pltpu.VMEM((experts, slot), jnp.int32),
            pltpu.VMEM((1, experts), jnp.int32),
            pltpu.VMEM((experts, 2, slot, width), HALF),
            pltpu.VMEM((nz, nx, 2, slot, width), HALF),
            pltpu.VMEM((nz, width, 2 * units), HALF),
            pltpu.VMEM((nz, 2 * units, width), HALF),
            pltpu.VMEM((ny, nz, 2, slot, 2 * units), HALF),
            pltpu.VMEM((ny, nz, 2, slot, 2 * units), HALF),
            pltpu.VMEM((2, nz, 2, slot, 2 * units), HALF),
            pltpu.VMEM((nz, ny, 2, slot, 2 * units), HALF),
            pltpu.VMEM((nz, 2, slot, 2 * units), HALF),
            pltpu.VMEM((nz, ny, slot, 2 * units), HALF),
            pltpu.VMEM((nx, slot, width), HALF),
            pltpu.VMEM((nx, slot, width), HALF),
            pltpu.VMEM((units, width), FULL),
            pltpu.VMEM((2, units, width), FULL),
            pltpu.VMEM((2, units, width), FULL),
            pltpu.VMEM((frames, grid_rows, columns, width), FULL),
            pltpu.VMEM((frames + 2, grid_rows + 2, columns, width), HALF),
            pltpu.VMEM((3, frames + 2, grid_rows + 2, columns, width), FULL),
            dma((6,)), dma((nx,)), dma((nx,)),
            dma((2,)), dma((2,)), dma((2,)),
            dma((4 * steps,)), dma((4 * steps,)), dma((4 * steps,)), dma((4 * steps,)),
            dma((8 * steps,)), dma((8 * steps,)),
            dma(((steps + 1) * ny,)), dma(((steps + 1) * ny,)),
            dma((nz,)), dma((nz,)),
            dma(((steps + 1) * ny,)), dma(((steps + 1) * ny,)),
            dma((2 * ny,)), dma((2 * ny,)),
            dma((nx,)), dma((nx,)),
            dma((2,)), dma((2,)),
            dma((8,)), dma((8,)),
        ],
        compiler_params=pltpu.CompilerParams(
            collective_id=0, has_side_effects=True, vmem_limit_bytes=62 * 1024 * 1024
        ),
    )(
        saved_conv.reshape(tokens, width),
        grad_out.reshape(tokens, width),
        conv_kernel,
        weight_in,
        weight_out,
        gate_values.reshape(gate_values.shape[1:]),
        picked_slots.reshape(experts, slot),
        slot_counts.reshape(1, experts),
    )
    return out, grad_in[None], grad_w[None]


def solution(mesh):
    placed = (
        P("tm", "height", None, "expert"),
        P("tm", "height", None, "expert"),
        P(None, "expert"),
        P(None, "expert", "height"),
        P(None, "height", "expert"),
        P("tm", None, None),
        P("tm", "height", None, None),
        P("tm", "height", None),
    )
    sizes = (mesh.shape["tm"], mesh.shape["height"], mesh.shape["expert"])
    return jax.shard_map(
        functools.partial(on_device, *sizes),
        mesh=mesh,
        in_specs=placed,
        out_specs=(
            P("tm", "height", None, "expert"),
            P("tm", "expert", "height"),
            P("tm", "height", "expert"),
        ),
        check_vma=False,
    )
```
